32 devices in a mesh: row: 4 (over y, x), col: 8 (over z, core).
Axes of the slice: x: 2, y: 2, z: 4, core: 2. Of those that a mesh axis runs over, the one named last changes fastest.
Arguments:
- traces: bfloat16 [64, 4096], P(None, ('row', 'col')), may hold values from -6 to 6
- incident: bfloat16 [64, 4096], P(None, ('row', 'col')), may hold values from -6 to 6
- points: float32 [3, 4096], P(None, ('row', 'col')), may hold values from 0 to 1
- coupling: int32 [4096], P(('row', 'col')), may hold values from 0 to 2047, as said below
- volume_tiles: bfloat16 [16, 32, 4, 128, 128], P('row', 'col'), may hold values from -0.125 to 0.125
- tile_columns: int32 [16, 32, 4], P('row', 'col'), may hold values from 0 to 8, as said below
Outputs:
- traces_out: bfloat16 [64, 4096], P(None, ('row', 'col'))
- volume_out: float32 [64, 16, 32, 128], P(None, 'row', 'col')
The draws below stay inside these ranges and needn't reach their ends.
Inputs may be any that keep to these rules, and one draw needn't show every extreme that they name: `coupling`: within each aligned block of 128 unknowns the values are distinct. `tile_columns`: the 4 entries of one tile are distinct, and one of them is 4.
All inputs are finite; a program needn't handle non-finite values.
Results may differ from the reference program's by a relative error of at most 0.0154.
Values may be sent and summed in bfloat16 or wider, within the bound.
A program may use at most 64 MiB of HBM per device.

```python
import math
import jax
import jax.numpy as jnp
from jax import lax

EXCITE = 64
SURF_DEV = 128
TILES_Y = 4
TILES_X = 4
TILE_SIDE = 128
TILE_COUNT = 4
OUTER_STEPS = 2
PASSES = 2
SURFACE = 4096
GRID_Y = 16
GRID_X = 32
N_ROW = 4
N_COL = 8


def draw_coupling(key, part):
    vol_rows = TILES_Y * TILES_X * TILE_SIDE
    block_count = SURFACE // SURF_DEV
    keys = jax.random.split(jax.random.fold_in(key, 7), block_count)

    def one_block(subkey):
        return jax.random.permutation(subkey, vol_rows)[:SURF_DEV]
    values = jax.vmap(one_block)(keys).astype(jnp.int32)
    inner = (jax.random.permutation(jax.random.fold_in(key, 8), vol_rows - 2)[:SURF_DEV - 2] + 1).astype(jnp.int32)
    ends = jnp.array([0, vol_rows - 1], jnp.int32)
    first_block = jax.random.permutation(jax.random.fold_in(key, 9), jnp.concatenate([ends, inner]))
    values = values.at[0].set(first_block)
    return values.reshape(SURFACE).astype(jnp.int32)


def draw_tile_columns(key, part):
    count_all = GRID_Y * GRID_X
    others = jnp.array([0, 1, 2, 3, 5, 6, 7, 8], jnp.int32)
    keys_pick = jax.random.split(jax.random.fold_in(key, 11), count_all)
    keys_order = jax.random.split(jax.random.fold_in(key, 12), count_all)

    def pick_others(subkey):
        return jax.random.permutation(subkey, others)[:TILE_COUNT - 1]
    picks = jax.vmap(pick_others)(keys_pick)
    centre = jnp.full((count_all, 1), 4, jnp.int32)
    full = jnp.concatenate([picks, centre], axis=1)

    def order_one(subkey):
        return jax.random.permutation(subkey, TILE_COUNT)
    order = jax.vmap(order_one)(keys_order)
    mixed = jnp.take_along_axis(full, order, axis=1)
    return mixed.reshape(GRID_Y, GRID_X, TILE_COUNT).astype(jnp.int32)


def shard_levels(own_key, dims, cuts, least, high):
    gain, own = 1.0, jax.random.fold_in(own_key, 6)
    for dim, parts in cuts:
        draws = jnp.exp(jax.random.uniform(jax.random.fold_in(own, dim), (parts,), jnp.float32, least / len(cuts), high / len(cuts)))
        gain = gain * jnp.repeat(draws, dims[dim] // parts).reshape([-1 if axis == dim else 1 for axis in range(len(dims))])
    return gain


def centred(rng, dims, scale, bound, shards=(), kind=jnp.bfloat16):
    drawn = jax.random.normal(rng, dims, jnp.float32) * scale
    if len(shards) > 0:
        drawn = shard_levels(rng, dims, shards, -0.22, 0.18) * drawn
    return jnp.clip(drawn, min=-bound, max=bound).astype(kind)


def setup_inputs(seed: int = 0) -> dict:
    splits = jax.random.split(jax.random.key(seed), 7)
    return {
        "traces": centred(splits[0], (EXCITE, SURFACE), 1.0, 6.0, ((1, 32),)),
        "incident": centred(splits[1], (EXCITE, SURFACE), 1.0, 6.0, ((1, 32),)),
        "points": jnp.clip(1.0 * jax.random.uniform(splits[2], (3, SURFACE), jnp.float32) ** shard_levels(splits[2], (3, SURFACE), ((1, 32),), -0.2, 0.2), 0.0, 1.0),
        "coupling": draw_coupling(jax.random.fold_in(splits[6], 71), 0),
        "volume_tiles": centred(splits[4], (GRID_Y, GRID_X, TILE_COUNT, TILE_SIDE, TILE_SIDE), (4 * TILE_COUNT * TILE_SIDE) ** -0.5, 0.125, ((0, 4), (1, 8))),
        "tile_columns": draw_tile_columns(jax.random.fold_in(splits[6], 71), 0),
    }


def wave_constants(total):
    spacing = float(total) ** (-1.0 / 3.0)
    return (2.0 / spacing, (0.5 * spacing) ** 2, 1.0 / math.sqrt(2.0 * total))

def kernel_block(source_points, target_points, consts):
    wave, smooth, factor = consts
    delta_x = source_points[0][:, None] - target_points[0][None, :]
    delta_y = source_points[1][:, None] - target_points[1][None, :]
    delta_z = source_points[2][:, None] - target_points[2][None, :]
    radius = jnp.sqrt(delta_x * delta_x + delta_y * delta_y + delta_z * delta_z + smooth)
    return (factor * jnp.cos(wave * radius) / radius).astype(jnp.bfloat16)

def apply_tiles(rounded, volume_tiles, tile_columns):
    padded = jnp.pad(rounded, ((0, 0), (1, 1), (1, 1), (0, 0)))
    picked = jnp.zeros(rounded.shape[:3] + (TILE_COUNT, TILE_SIDE), jnp.bfloat16)
    for offset in range(9):
        first = offset // 3
        second = offset % 3
        view = padded[:, first:first + GRID_Y, second:second + GRID_X, :]
        picked = jnp.where((tile_columns == offset)[None, :, :, :, None], view[:, :, :, None, :], picked)
    return jnp.einsum('eyxkq,yxkpq->eyxp', picked.astype(jnp.float32), volume_tiles.astype(jnp.float32))

def to_grid(local_rows):
    shaped = local_rows.reshape(EXCITE, N_ROW, N_COL, TILES_Y, TILES_X, TILE_SIDE)
    return shaped.transpose(0, 1, 3, 2, 4, 5).reshape(EXCITE, GRID_Y, GRID_X, TILE_SIDE)

def from_grid(field):
    shaped = field.reshape(EXCITE, N_ROW, TILES_Y, N_COL, TILES_X, TILE_SIDE)
    return shaped.transpose(0, 1, 3, 2, 4, 5).reshape(EXCITE, N_ROW, N_COL, TILES_Y * TILES_X * TILE_SIDE)

def reference(traces, incident, points, coupling, volume_tiles, tile_columns):
    consts = wave_constants(SURFACE)
    block_len = min(256, SURFACE)
    block_count = SURFACE // block_len
    target_blocks = points.reshape(3, block_count, block_len).transpose(1, 0, 2)
    row_index = jnp.arange(N_ROW, dtype=jnp.int32)[:, None, None]
    col_index = jnp.arange(N_COL, dtype=jnp.int32)[None, :, None]
    couple_grid = coupling.reshape(N_ROW, N_COL, SURF_DEV).astype(jnp.int32)
    vol_rows = TILES_Y * TILES_X * TILE_SIDE
    present = traces
    field = jnp.zeros((EXCITE, GRID_Y, GRID_X, TILE_SIDE), jnp.float32)
    for outer in range(OUTER_STEPS):

        def one_block(targets, present=present):
            kernel = kernel_block(points, targets, consts)
            return jnp.dot(present, kernel, preferred_element_type=jnp.float32)
        currents = lax.map(one_block, target_blocks)
        currents = currents.transpose(1, 0, 2).reshape(EXCITE, N_ROW, N_COL, SURF_DEV)
        local_source = jnp.zeros((EXCITE, N_ROW, N_COL, vol_rows), jnp.float32)
        local_source = local_source.at[:, row_index, col_index, couple_grid].set(currents)
        source = to_grid(local_source)
        field = source
        for sweep in range(PASSES):
            rounded = field.astype(jnp.bfloat16)
            field = source + apply_tiles(rounded, volume_tiles, tile_columns)
        readout = from_grid(field)[:, row_index, col_index, couple_grid].reshape(EXCITE, SURFACE)
        present = (incident.astype(jnp.float32) + readout).astype(jnp.bfloat16)
    return (present, field)
```

```python
import functools
import math

import jax
import jax.numpy as jnp
import numpy as np
from jax import lax
from jax.experimental import pallas as pl
from jax.experimental.pallas import tpu as pltpu
from jax.sharding import PartitionSpec as P

OUTER_STEPS = 2
MESH = pl.DeviceIdType.MESH
NEIGHBOURS = ((-1, 0), (1, 0), (-1, -1), (-1, 1), (1, -1), (1, 1), (0, -1), (0, 1))
CHUNK = 16


def cosine_terms(degree):
    grid = 0.125 * (1.0 - np.cos(np.pi * (np.arange(400) + 0.5) / 400))
    fit = np.polynomial.Chebyshev.fit(grid, np.cos(2 * np.pi * np.sqrt(grid)), degree, domain=[0, 0.25])
    return [float(term) for term in fit.convert(kind=np.polynomial.Polynomial).coef]


def slot_of(dy, dx):
    return (dy + 1) * 3 + dx + 1


def edge_range(step, size):
    if step == 0:
        return list(range(size))
    return [size - 1] if step < 0 else [0]


def body(
    n_row, n_col, total, tiles_y, tiles_x, tile_count,
    columns, traces, incident, points, coupling, volume,
    traces_out, field_out,
    meta_own, meta_plane, meta_z, meta_halo, cols, kernel, hot_own, hot_halo, tiles,
    pres, gath, part, parts_in, curr, curr_halo, source, padded, own_one, pad_two, own_two, flat,
    load_sem, meta_plane_s, meta_plane_r, meta_z_s, meta_z_r, meta_halo_s, meta_halo_r,
    gath_s, gath_r, part_s, part_r, curr_s, curr_r, field_s, field_r,
):
    excite, shard = traces.shape
    group, depth = 2 * n_row, n_col // 2
    row, col = lax.axis_index("row"), lax.axis_index("col")
    z, core = col // 2, col % 2
    place = row * 2 + core
    wide = tiles_x + 2

    def plane_peer(step):
        other = (place + step) % group
        return (other // 2, z * 2 + other % 2)

    def z_peer(step):
        return (row, ((z + step) % depth) * 2 + core)

    def has(dy, dx):
        fine = None
        for step, index, size in ((dy, row, n_row), (dx, col, n_col)):
            if step != 0:
                good = index > 0 if step < 0 else index < size - 1
                fine = good if fine is None else jnp.logical_and(fine, good)
        return fine

    def send(src, dst, send_sem, recv_sem, device):
        return pltpu.make_async_remote_copy(
            src_ref=src, dst_ref=dst, send_sem=send_sem, recv_sem=recv_sem,
            device_id=device, device_id_type=MESH,
        )

    load = pltpu.make_async_copy(volume, tiles, load_sem)
    load.start()

    meta_halo[...] = jnp.zeros_like(meta_halo)
    curr_halo[...] = jnp.zeros_like(curr_halo)
    for outer in range(OUTER_STEPS):
        for y in range(tiles_y + 2):
            for x in range(tiles_x + 2):
                if y in (0, tiles_y + 1) or x in (0, tiles_x + 1):
                    pad_two[outer, y, x] = jnp.zeros((excite, shard), jnp.bfloat16)
    meta_own[...] = jnp.concatenate(
        [points[...], coupling[...].astype(jnp.float32), jnp.zeros((4, shard), jnp.float32)], axis=0
    )
    pres[0] = traces[...]
    meta_plane[0] = meta_own[...]
    meta_z[0] = meta_own[...]
    gath[0, 0] = traces[...]

    barrier = pltpu.get_barrier_semaphore()

    def greet(device):
        pl.semaphore_signal(barrier, inc=1, device_id=device, device_id_type=MESH)

    for step in range(1, group):
        greet(plane_peer(step))
    for step in range(1, depth):
        greet(z_peer(step))
    expected = jnp.int32(group - 1 + depth - 1)
    for dy, dx in NEIGHBOURS:
        there = has(dy, dx)
        pl.when(there)(functools.partial(greet, (row + dy, col + dx)))
        expected = expected + jnp.where(there, 1, 0)
    pl.semaphore_wait(barrier, expected)

    def meta_plane_copy(step):
        return send(meta_own, meta_plane.at[step], meta_plane_s.at[step], meta_plane_r.at[step], plane_peer(step))

    def meta_z_copy(step):
        return send(meta_own, meta_z.at[step], meta_z_s.at[step], meta_z_r.at[step], z_peer(step))

    def meta_halo_copy(dy, dx):
        mine, theirs = slot_of(dy, dx), slot_of(-dy, -dx)
        return send(meta_own, meta_halo.at[theirs], meta_halo_s.at[mine], meta_halo_r.at[theirs], (row + dy, col + dx))

    def meta_halo_arrival(dy, dx):
        mine = slot_of(dy, dx)
        return send(meta_own, meta_halo.at[mine], meta_halo_s.at[mine], meta_halo_r.at[mine], (row + dy, col + dx))

    def gath_copy(outer, step):
        return send(pres.at[outer], gath.at[outer, step], gath_s.at[outer, step], gath_r.at[outer, step], plane_peer(step))

    def part_copy(outer, step):
        return send(part.at[outer, step], parts_in.at[outer, step], part_s.at[outer, step], part_r.at[outer, step], z_peer(-step))

    def curr_copy(outer, dy, dx, slot):
        return send(
            curr.at[outer], curr_halo.at[outer, slot], curr_s.at[outer, slot_of(dy, dx)],
            curr_r.at[outer, slot], (row + dy, col + dx),
        )

    def field_copy(outer, dy, dx, arrival):
        side = (dy, dx) if arrival else (-dy, -dx)
        ranges, sources = [], []
        for step, out_step, size in ((side[0], dy, tiles_y), (side[1], dx, tiles_x)):
            ranges.append(pl.ds(1, size) if step == 0 else pl.ds(0 if step < 0 else size + 1, 1))
            sources.append(pl.ds(0, size) if out_step == 0 else pl.ds(0 if out_step < 0 else size - 1, 1))
        slot = slot_of(*side)
        return send(
            own_two.at[outer, sources[0], sources[1]], pad_two.at[outer, ranges[0], ranges[1]],
            field_s.at[outer, slot_of(dy, dx)], field_r.at[outer, slot], (row + dy, col + dx),
        )

    for step in range(1, group):
        meta_plane_copy(step).start()
    for step in range(1, depth):
        meta_z_copy(step).start()
    for step in range(1, group):
        gath_copy(0, step).start()
    for dy, dx in NEIGHBOURS:
        pl.when(has(dy, dx))(lambda dy=dy, dx=dx: meta_halo_copy(dy, dx).start())

    lanes = lax.broadcasted_iota(jnp.int32, (shard, shard), 1).astype(jnp.float32)

    def one_hot(column, tile):
        return jnp.where(column == lanes + float(tile * shard), 1.0, 0.0).astype(jnp.bfloat16)

    own_column = jnp.broadcast_to(meta_own[...].T[:, 3:4], (shard, shard))
    for tile in range(tiles_y * tiles_x):
        hot_own[:, tile * shard:(tile + 1) * shard] = one_hot(own_column, tile)

    for step in range(1, group):
        meta_plane_copy(step).wait_recv()
    for step in range(1, depth):
        meta_z_copy(step).wait_recv()

    wave = 2.0 * float(total) ** (1.0 / 3.0)
    smooth = (0.5 * float(total) ** (-1.0 / 3.0)) ** 2
    factor = 1.0 / math.sqrt(2.0 * total)
    terms = [factor * term for term in cosine_terms(5)]
    for step in range(group):
        cols[step * shard:(step + 1) * shard, :] = meta_plane[step].T
    targets = [jnp.concatenate([meta_z[step, d:d + 1, :] for step in range(depth)], axis=1) for d in range(3)]

    def build(number, carry):
        rows = pl.ds(pl.multiple_of(number * CHUNK, CHUNK), CHUNK)
        mine = cols[rows, :]
        square = smooth
        for d in range(3):
            delta = mine[:, d:d + 1] - targets[d]
            square = square + delta * delta
        inverse = lax.rsqrt(square)
        turns = (wave / (2.0 * math.pi)) * (square * inverse)
        turns = turns - jnp.floor(turns + 0.5)
        turns = turns * turns
        value = terms[-1]
        for term in terms[-2::-1]:
            value = value * turns + term
        kernel[rows, :] = (value * inverse).astype(jnp.bfloat16)
        return carry

    lax.fori_loop(0, group * shard // CHUNK, build, 0, unroll=2)

    halo_places, number = {}, 0
    for dy, dx in NEIGHBOURS:
        pl.when(has(dy, dx))(lambda dy=dy, dx=dx: meta_halo_arrival(dy, dx).wait_recv())
        column = jnp.broadcast_to(meta_halo[slot_of(dy, dx)].T[:, 3:4], (shard, shard))
        places = []
        for y in edge_range(dy, tiles_y):
            for x in edge_range(dx, tiles_x):
                hot_halo[:, number * shard:(number + 1) * shard] = one_hot(column, y * tiles_x + x)
                to_y = y + 1 if dy == 0 else (0 if dy < 0 else tiles_y + 1)
                to_x = x + 1 if dx == 0 else (0 if dx < 0 else tiles_x + 1)
                places.append((number, to_y, to_x))
                number += 1
        halo_places[(dy, dx)] = places

    load.wait()

    def pick(ref_index, ref, y, x, stride, shift):
        picked = []
        for k in range(tile_count):
            offset = columns[(y * tiles_x + x) * tile_count + k]
            at = (y + offset // 3 - shift) * stride + x + offset % 3 - shift
            picked.append(ref[at] if ref_index is None else ref[ref_index, at])
        return jnp.concatenate(picked, axis=1)

    def apply(picked, y, x):
        acc = source[y * tiles_x + x]
        for k in range(tile_count):
            acc = acc + lax.dot_general(
                picked[:, k * shard:(k + 1) * shard], tiles[y, x, k], (((1,), (1,)), ((), ())),
                preferred_element_type=jnp.float32,
            )
        return acc

    inner = [(y, x) for y in range(1, tiles_y - 1) for x in range(1, tiles_x - 1)]
    outside = [(y, x) for y in range(tiles_y) for x in range(tiles_x) if (y, x) not in inner]

    def outer_step(outer):
        for step in range(1, group):
            gath_copy(outer, step).wait_recv()
        gathered = jnp.concatenate([gath[outer, step] for step in range(group)], axis=1)
        sums = jnp.dot(gathered, kernel[...], preferred_element_type=jnp.float32)
        for step in range(1, depth):
            part[outer, step] = sums[:, step * shard:(step + 1) * shard].astype(jnp.bfloat16)
        for step in range(1, depth):
            part_copy(outer, step).start()
        current = sums[:, :shard]
        for step in range(1, depth):
            part_copy(outer, step).wait_recv()
            current = current + parts_in[outer, step].astype(jnp.float32)
        rounded = current.astype(jnp.bfloat16)
        curr[outer] = rounded
        for dy, dx in NEIGHBOURS:
            pl.when(has(dy, dx))(lambda dy=dy, dx=dx: curr_copy(outer, dy, dx, slot_of(-dy, -dx)).start())

        spread = jnp.dot(rounded, hot_own[...], preferred_element_type=jnp.float32)
        for y in range(tiles_y):
            for x in range(tiles_x):
                tile = y * tiles_x + x
                value = spread[:, tile * shard:(tile + 1) * shard]
                source[tile] = value
                value = value.astype(jnp.bfloat16)
                padded[(y + 1) * wide + x + 1] = value
                own_one[tile] = value
        for y, x in inner:
            own_two[outer, y, x] = apply(pick(None, own_one, y, x, tiles_x, 1), y, x).astype(jnp.bfloat16)
        for dy, dx in NEIGHBOURS:
            pl.when(has(dy, dx))(lambda dy=dy, dx=dx: curr_copy(outer, dy, dx, slot_of(dy, dx)).wait_recv())
            places = halo_places[(dy, dx)]
            first = places[0][0]
            halo = jnp.dot(
                curr_halo[outer, slot_of(dy, dx)], hot_halo[:, first * shard:(first + len(places)) * shard],
                preferred_element_type=jnp.float32,
            ).astype(jnp.bfloat16)
            for number, y, x in places:
                padded[y * wide + x] = halo[:, (number - first) * shard:(number - first + 1) * shard]
        for y, x in outside:
            own_two[outer, y, x] = apply(pick(None, padded, y, x, wide, 0), y, x).astype(jnp.bfloat16)
        for dy, dx in NEIGHBOURS:
            pl.when(has(dy, dx))(lambda dy=dy, dx=dx: field_copy(outer, dy, dx, False).start())
        for y in range(tiles_y):
            for x in range(tiles_x):
                value = own_two[outer, y, x]
                own_one[y * tiles_x + x] = value
                padded[(y + 1) * wide + x + 1] = value

        def finish(ref, y, x, stride, shift):
            tile = y * tiles_x + x
            value = apply(pick(None, ref, y, x, stride, shift), y, x)
            field_out[tile] = value
            flat[:, tile * shard:(tile + 1) * shard] = value.astype(jnp.bfloat16)

        for y, x in inner:
            finish(own_one, y, x, tiles_x, 1)
        for dy, dx in NEIGHBOURS:
            pl.when(has(dy, dx))(lambda dy=dy, dx=dx: field_copy(outer, dy, dx, True).wait_recv())
        for y in range(tiles_y + 2):
            for x in range(tiles_x + 2):
                if y in (0, tiles_y + 1) or x in (0, tiles_x + 1):
                    padded[y * wide + x] = pad_two[outer, y, x]
        for y, x in outside:
            finish(padded, y, x, wide, 0)
        readout = lax.dot_general(
            flat[...], hot_own[...], (((1,), (1,)), ((), ())), preferred_element_type=jnp.float32
        )
        present = (incident[...].astype(jnp.float32) + readout).astype(jnp.bfloat16)
        traces_out[...] = present

        if outer + 1 < OUTER_STEPS:
            pres[outer + 1] = present
            gath[outer + 1, 0] = present
            for step in range(1, group):
                gath_copy(outer + 1, step).start()

        for step in range(1, group):
            gath_copy(outer, step).wait_send()
        for step in range(1, depth):
            part_copy(outer, step).wait_send()
        for dy, dx in NEIGHBOURS:
            pl.when(has(dy, dx))(lambda dy=dy, dx=dx: curr_copy(outer, dy, dx, slot_of(-dy, -dx)).wait_send())
            pl.when(has(dy, dx))(lambda dy=dy, dx=dx: field_copy(outer, dy, dx, False).wait_send())

    for outer in range(OUTER_STEPS):
        outer_step(outer)
    for step in range(1, group):
        meta_plane_copy(step).wait_send()
    for step in range(1, depth):
        meta_z_copy(step).wait_send()
    for dy, dx in NEIGHBOURS:
        pl.when(has(dy, dx))(lambda dy=dy, dx=dx: meta_halo_copy(dy, dx).wait_send())


def per_device(n_row, n_col, traces, incident, points, coupling, volume_tiles, tile_columns):
    excite, shard = traces.shape
    total = shard * n_row * n_col
    tiles_y, tiles_x, tile_count, side, _ = volume_tiles.shape
    group, depth = 2 * n_row, n_col // 2
    count = tiles_y * tiles_x
    halo = 2 * (tiles_y + tiles_x) + 4
    dma = pltpu.SemaphoreType.DMA
    bf16, f32 = jnp.bfloat16, jnp.float32
    vmem = pl.BlockSpec(memory_space=pltpu.VMEM)
    steps = OUTER_STEPS
    present, field = pl.pallas_call(
        functools.partial(body, n_row, n_col, total, tiles_y, tiles_x, tile_count),
        out_shape=(
            jax.ShapeDtypeStruct((excite, shard), bf16),
            jax.ShapeDtypeStruct((count, excite, side), f32),
        ),
        in_specs=[pl.BlockSpec(memory_space=pltpu.SMEM), vmem, vmem, vmem, vmem, pl.BlockSpec(memory_space=pl.ANY)],
        out_specs=(vmem, vmem),
        scratch_shapes=[
            pltpu.VMEM((8, shard), f32),
            pltpu.VMEM((group, 8, shard), f32),
            pltpu.VMEM((depth, 8, shard), f32),
            pltpu.VMEM((9, 8, shard), f32),
            pltpu.VMEM((group * shard, 8), f32),
            pltpu.VMEM((group * shard, depth * shard), bf16),
            pltpu.VMEM((shard, count * side), bf16),
            pltpu.VMEM((shard, halo * side), bf16),
            pltpu.VMEM(volume_tiles.shape, bf16),
            pltpu.VMEM((steps, excite, shard), bf16),
            pltpu.VMEM((steps, group, excite, shard), bf16),
            pltpu.VMEM((steps, depth, excite, shard), bf16),
            pltpu.VMEM((steps, depth, excite, shard), bf16),
            pltpu.VMEM((steps, excite, shard), bf16),
            pltpu.VMEM((steps, 9, excite, shard), bf16),
            pltpu.VMEM((count, excite, side), f32),
            pltpu.VMEM(((tiles_y + 2) * (tiles_x + 2), excite, side), bf16),
            pltpu.VMEM((count, excite, side), bf16),
            pltpu.VMEM((steps, tiles_y + 2, tiles_x + 2, excite, side), bf16),
            pltpu.VMEM((steps, tiles_y, tiles_x, excite, side), bf16),
            pltpu.VMEM((excite, count * side), bf16),
            dma, dma((group,)), dma((group,)), dma((depth,)), dma((depth,)), dma((9,)), dma((9,)),
            dma((steps, group)), dma((steps, group)), dma((steps, depth)), dma((steps, depth)),
            dma((steps, 9)), dma((steps, 9)), dma((steps, 9)), dma((steps, 9)),
        ],
        compiler_params=pltpu.CompilerParams(
            collective_id=0, has_side_effects=True, vmem_limit_bytes=40 * 2**20
        ),
        cost_estimate=pl.CostEstimate(flops=10**9, bytes_accessed=4 * 2**20, transcendentals=0),
    )(tile_columns.reshape(-1), traces, incident, points, coupling.reshape(1, shard), volume_tiles)
    field = field.reshape(tiles_y, tiles_x, excite, side).transpose(2, 0, 1, 3)
    return (present, field)


def solution(mesh):
    in_specs = (
        P(None, ("row", "col")),
        P(None, ("row", "col")),
        P(None, ("row", "col")),
        P(("row", "col")),
        P("row", "col", None, None, None),
        P("row", "col", None),
    )
    out_specs = (P(None, ("row", "col")), P(None, "row", "col", None))
    return jax.shard_map(
        functools.partial(per_device, mesh.shape["row"], mesh.shape["col"]),
        mesh=mesh, in_specs=in_specs, out_specs=out_specs, check_vma=False,
    )
```

```python
import functools
import math

import jax
import jax.numpy as jnp
import numpy as np
from jax import lax
from jax.experimental import pallas as pl
from jax.experimental.pallas import tpu as pltpu
from jax.sharding import PartitionSpec as P

OUTER_STEPS = 2
MESH = pl.DeviceIdType.MESH
NEIGHBOURS = ((-1, 0), (1, 0), (-1, -1), (-1, 1), (1, -1), (1, 1), (0, -1), (0, 1))
CHUNK = 16


def cosine_terms(degree):
    grid = 0.125 * (1.0 - np.cos(np.pi * (np.arange(400) + 0.5) / 400))
    fit = np.polynomial.Chebyshev.fit(grid, np.cos(2 * np.pi * np.sqrt(grid)), degree, domain=[0, 0.25])
    return [float(term) for term in fit.convert(kind=np.polynomial.Polynomial).coef]


def slot_of(dy, dx):
    return (dy + 1) * 3 + dx + 1


def edge_range(step, size):
    if step == 0:
        return list(range(size))
    return [size - 1] if step < 0 else [0]


def body(
    n_row, n_col, total, tiles_y, tiles_x, tile_count,
    columns, traces, incident_in, points_in, coupling_in, volume,
    traces_out, field_out,
    incident, points, coupling, hot_read, meta_own, meta_plane, meta_z, meta_halo, cols, kernel, hot_own, hot_halo, tiles,
    pres, gath, part, parts_in, curr, curr_halo, source, padded, own_one, pad_two, own_two, flat,
    load_sem, small_sem, meta_plane_s, meta_plane_r, meta_z_s, meta_z_r, meta_halo_s, meta_halo_r,
    gath_s, gath_r, part_s, part_r, curr_s, curr_r, field_s, field_r,
):
    excite, shard = traces.shape
    group, depth = 2 * n_row, n_col // 2
    row, col = lax.axis_index("row"), lax.axis_index("col")
    z, core = col // 2, col % 2
    place = row * 2 + core
    wide = tiles_x + 2

    def plane_peer(step):
        other = (place + step) % group
        return (other // 2, z * 2 + other % 2)

    def z_peer(step):
        return (row, ((z + step) % depth) * 2 + core)

    def has(dy, dx):
        fine = None
        for step, index, size in ((dy, row, n_row), (dx, col, n_col)):
            if step != 0:
                good = index > 0 if step < 0 else index < size - 1
                fine = good if fine is None else jnp.logical_and(fine, good)
        return fine

    def send(src, dst, send_sem, recv_sem, device):
        return pltpu.make_async_remote_copy(
            src_ref=src, dst_ref=dst, send_sem=send_sem, recv_sem=recv_sem,
            device_id=device, device_id_type=MESH,
        )

    load = pltpu.make_async_copy(volume, tiles, load_sem)
    small = [
        pltpu.make_async_copy(src, dst, small_sem.at[number])
        for number, (src, dst) in enumerate((
            (traces, pres.at[0]), (points_in, points), (coupling_in, coupling), (incident_in, incident),
        ))
    ]
    for copy in small:
        copy.start()
    load.start()

    meta_halo[...] = jnp.zeros_like(meta_halo)
    curr_halo[...] = jnp.zeros_like(curr_halo)
    for outer in range(OUTER_STEPS):
        for y in range(tiles_y + 2):
            for x in range(tiles_x + 2):
                if y in (0, tiles_y + 1) or x in (0, tiles_x + 1):
                    pad_two[outer, y, x] = jnp.zeros((excite, shard), jnp.bfloat16)
    for copy in small:
        copy.wait()
    meta_own[...] = jnp.concatenate(
        [points[...], coupling[...].astype(jnp.float32), jnp.zeros((4, shard), jnp.float32)], axis=0
    )
    meta_plane[0] = meta_own[...]
    meta_z[0] = meta_own[...]
    gath[0, 0] = pres[0]

    barrier = pltpu.get_barrier_semaphore()

    def greet(device):
        pl.semaphore_signal(barrier, inc=1, device_id=device, device_id_type=MESH)

    for step in range(1, group):
        greet(plane_peer(step))
    for step in range(1, depth):
        greet(z_peer(step))
    expected = jnp.int32(group - 1 + depth - 1)
    for dy, dx in NEIGHBOURS:
        there = has(dy, dx)
        pl.when(there)(functools.partial(greet, (row + dy, col + dx)))
        expected = expected + jnp.where(there, 1, 0)
    pl.semaphore_wait(barrier, expected)

    def meta_plane_copy(step):
        return send(meta_own, meta_plane.at[step], meta_plane_s.at[step], meta_plane_r.at[step], plane_peer(step))

    def meta_z_copy(step):
        return send(meta_own, meta_z.at[step], meta_z_s.at[step], meta_z_r.at[step], z_peer(step))

    def meta_halo_copy(dy, dx):
        mine, theirs = slot_of(dy, dx), slot_of(-dy, -dx)
        return send(meta_own, meta_halo.at[theirs], meta_halo_s.at[mine], meta_halo_r.at[theirs], (row + dy, col + dx))

    def meta_halo_arrival(dy, dx):
        mine = slot_of(dy, dx)
        return send(meta_own, meta_halo.at[mine], meta_halo_s.at[mine], meta_halo_r.at[mine], (row + dy, col + dx))

    def gath_copy(outer, step):
        return send(pres.at[outer], gath.at[outer, step], gath_s.at[outer, step], gath_r.at[outer, step], plane_peer(step))

    def part_copy(outer, step):
        return send(part.at[outer, step], parts_in.at[outer, step], part_s.at[outer, step], part_r.at[outer, step], z_peer(-step))

    def curr_copy(outer, dy, dx, slot):
        return send(
            curr.at[outer], curr_halo.at[outer, slot], curr_s.at[outer, slot_of(dy, dx)],
            curr_r.at[outer, slot], (row + dy, col + dx),
        )

    def field_copy(outer, dy, dx, arrival):
        side = (dy, dx) if arrival else (-dy, -dx)
        ranges, sources = [], []
        for step, out_step, size in ((side[0], dy, tiles_y), (side[1], dx, tiles_x)):
            ranges.append(pl.ds(1, size) if step == 0 else pl.ds(0 if step < 0 else size + 1, 1))
            sources.append(pl.ds(0, size) if out_step == 0 else pl.ds(0 if out_step < 0 else size - 1, 1))
        slot = slot_of(*side)
        return send(
            own_two.at[outer, sources[0], sources[1]], pad_two.at[outer, ranges[0], ranges[1]],
            field_s.at[outer, slot_of(dy, dx)], field_r.at[outer, slot], (row + dy, col + dx),
        )

    for step in range(1, group):
        meta_plane_copy(step).start()
    for step in range(1, depth):
        meta_z_copy(step).start()
    for step in range(1, group):
        gath_copy(0, step).start()
    for dy, dx in NEIGHBOURS:
        pl.when(has(dy, dx))(lambda dy=dy, dx=dx: meta_halo_copy(dy, dx).start())

    lanes = lax.broadcasted_iota(jnp.int32, (shard, shard), 1).astype(jnp.float32)

    def one_hot(column, tile):
        return jnp.where(column == lanes + float(tile * shard), 1.0, 0.0).astype(jnp.bfloat16)

    rows_of = lax.broadcasted_iota(jnp.int32, (shard, shard), 0)
    own_row = jnp.broadcast_to(coupling[...], (shard, shard))
    for tile in range(tiles_y * tiles_x):
        hot_read[tile * shard:(tile + 1) * shard, :] = jnp.where(
            own_row == rows_of + tile * shard, 1.0, 0.0
        ).astype(jnp.bfloat16)
    own_column = jnp.broadcast_to(meta_own[...].T[:, 3:4], (shard, shard))
    for tile in range(tiles_y * tiles_x):
        hot_own[:, tile * shard:(tile + 1) * shard] = one_hot(own_column, tile)

    for step in range(1, group):
        meta_plane_copy(step).wait_recv()
    for step in range(1, depth):
        meta_z_copy(step).wait_recv()

    wave = 2.0 * float(total) ** (1.0 / 3.0)
    smooth = (0.5 * float(total) ** (-1.0 / 3.0)) ** 2
    factor = 1.0 / math.sqrt(2.0 * total)
    terms = [factor * term for term in cosine_terms(5)]
    for step in range(group):
        cols[step * shard:(step + 1) * shard, :] = meta_plane[step].T
    targets = [jnp.concatenate([meta_z[step, d:d + 1, :] for step in range(depth)], axis=1) for d in range(3)]

    def build(number, carry):
        rows = pl.ds(pl.multiple_of(number * CHUNK, CHUNK), CHUNK)
        mine = cols[rows, :]
        square = smooth
        for d in range(3):
            delta = mine[:, d:d + 1] - targets[d]
            square = square + delta * delta
        inverse = lax.rsqrt(square)
        turns = (wave / (2.0 * math.pi)) * (square * inverse)
        turns = turns - jnp.floor(turns + 0.5)
        turns = turns * turns
        value = terms[-1]
        for term in terms[-2::-1]:
            value = value * turns + term
        kernel[rows, :] = (value * inverse).astype(jnp.bfloat16)
        return carry

    lax.fori_loop(0, group * shard // CHUNK, build, 0, unroll=2)

    halo_places, number = {}, 0
    for dy, dx in NEIGHBOURS:
        pl.when(has(dy, dx))(lambda dy=dy, dx=dx: meta_halo_arrival(dy, dx).wait_recv())
        column = jnp.broadcast_to(meta_halo[slot_of(dy, dx)].T[:, 3:4], (shard, shard))
        places = []
        for y in edge_range(dy, tiles_y):
            for x in edge_range(dx, tiles_x):
                hot_halo[:, number * shard:(number + 1) * shard] = one_hot(column, y * tiles_x + x)
                to_y = y + 1 if dy == 0 else (0 if dy < 0 else tiles_y + 1)
                to_x = x + 1 if dx == 0 else (0 if dx < 0 else tiles_x + 1)
                places.append((number, to_y, to_x))
                number += 1
        halo_places[(dy, dx)] = places

    load.wait()

    def apply(ref, y, x):
        tile = y * tiles_x + x
        picked = jnp.concatenate([ref[columns[tile * tile_count + k]] for k in range(tile_count)], axis=1)
        matrix = jnp.concatenate([tiles[y, x, k] for k in range(tile_count)], axis=1)
        return source[tile] + lax.dot_general(
            picked, matrix, (((1,), (1,)), ((), ())), preferred_element_type=jnp.float32
        )

    inner = [(y, x) for y in range(1, tiles_y - 1) for x in range(1, tiles_x - 1)]
    outside = [(y, x) for y in range(tiles_y) for x in range(tiles_x) if (y, x) not in inner]

    def outer_step(outer):
        for step in range(1, group):
            gath_copy(outer, step).wait_recv()
        gathered = jnp.concatenate([gath[outer, step] for step in range(group)], axis=1)
        sums = jnp.dot(gathered, kernel[...], preferred_element_type=jnp.float32)
        for step in range(1, depth):
            part[outer, step] = sums[:, step * shard:(step + 1) * shard].astype(jnp.bfloat16)
        for step in range(1, depth):
            part_copy(outer, step).start()
        current = sums[:, :shard]
        for step in range(1, depth):
            part_copy(outer, step).wait_recv()
            current = current + parts_in[outer, step].astype(jnp.float32)
        rounded = current.astype(jnp.bfloat16)
        curr[outer] = rounded
        for dy, dx in NEIGHBOURS:
            pl.when(has(dy, dx))(lambda dy=dy, dx=dx: curr_copy(outer, dy, dx, slot_of(-dy, -dx)).start())

        spread = jnp.dot(rounded, hot_own[...], preferred_element_type=jnp.float32)
        for y in range(tiles_y):
            for x in range(tiles_x):
                tile = y * tiles_x + x
                value = spread[:, tile * shard:(tile + 1) * shard]
                source[tile] = value
                value = value.astype(jnp.bfloat16)
                padded[(y + 1) * wide + x + 1] = value
                own_one[(y + 1) * wide + x + 1] = value
        for y, x in inner:
            own_two[outer, y, x] = apply(own_one, y, x).astype(jnp.bfloat16)
        for dy, dx in NEIGHBOURS:
            pl.when(has(dy, dx))(lambda dy=dy, dx=dx: curr_copy(outer, dy, dx, slot_of(dy, dx)).wait_recv())
            places = halo_places[(dy, dx)]
            first = places[0][0]
            halo = jnp.dot(
                curr_halo[outer, slot_of(dy, dx)], hot_halo[:, first * shard:(first + len(places)) * shard],
                preferred_element_type=jnp.float32,
            ).astype(jnp.bfloat16)
            for number, y, x in places:
                padded[y * wide + x] = halo[:, (number - first) * shard:(number - first + 1) * shard]
        for sideways in (False, True):
            for y, x in outside:
                if (y in (0, tiles_y - 1)) != sideways:
                    own_two[outer, y, x] = apply(padded, y, x).astype(jnp.bfloat16)
            for dy, dx in NEIGHBOURS:
                if (dy == 0) == sideways:
                    pl.when(has(dy, dx))(lambda dy=dy, dx=dx: field_copy(outer, dy, dx, False).start())
        for y in range(tiles_y):
            for x in range(tiles_x):
                value = own_two[outer, y, x]
                own_one[(y + 1) * wide + x + 1] = value
                padded[(y + 1) * wide + x + 1] = value

        def finish(ref, y, x):
            tile = y * tiles_x + x
            value = apply(ref, y, x)
            field_out[tile] = value
            flat[:, tile * shard:(tile + 1) * shard] = value.astype(jnp.bfloat16)

        for y, x in inner:
            finish(own_one, y, x)
        for dy, dx in NEIGHBOURS:
            pl.when(has(dy, dx))(lambda dy=dy, dx=dx: field_copy(outer, dy, dx, True).wait_recv())
        for y in range(tiles_y + 2):
            for x in range(tiles_x + 2):
                if y in (0, tiles_y + 1) or x in (0, tiles_x + 1):
                    padded[y * wide + x] = pad_two[outer, y, x]
        for y, x in outside:
            finish(padded, y, x)
        readout = jnp.dot(flat[...], hot_read[...], preferred_element_type=jnp.float32)
        present = (incident[...].astype(jnp.float32) + readout).astype(jnp.bfloat16)
        traces_out[...] = present

        if outer + 1 < OUTER_STEPS:
            pres[outer + 1] = present
            gath[outer + 1, 0] = present
            for step in range(1, group):
                gath_copy(outer + 1, step).start()

        for step in range(1, group):
            gath_copy(outer, step).wait_send()
        for step in range(1, depth):
            part_copy(outer, step).wait_send()
        for dy, dx in NEIGHBOURS:
            pl.when(has(dy, dx))(lambda dy=dy, dx=dx: curr_copy(outer, dy, dx, slot_of(-dy, -dx)).wait_send())
            pl.when(has(dy, dx))(lambda dy=dy, dx=dx: field_copy(outer, dy, dx, False).wait_send())

    for outer in range(OUTER_STEPS):
        outer_step(outer)
    for step in range(1, group):
        meta_plane_copy(step).wait_send()
    for step in range(1, depth):
        meta_z_copy(step).wait_send()
    for dy, dx in NEIGHBOURS:
        pl.when(has(dy, dx))(lambda dy=dy, dx=dx: meta_halo_copy(dy, dx).wait_send())


def per_device(n_row, n_col, traces, incident, points, coupling, volume_tiles, tile_columns):
    excite, shard = traces.shape
    total = shard * n_row * n_col
    tiles_y, tiles_x, tile_count, side, _ = volume_tiles.shape
    group, depth = 2 * n_row, n_col // 2
    count = tiles_y * tiles_x
    halo = 2 * (tiles_y + tiles_x) + 4
    dma = pltpu.SemaphoreType.DMA
    bf16, f32 = jnp.bfloat16, jnp.float32
    vmem = pl.BlockSpec(memory_space=pltpu.VMEM)
    steps = OUTER_STEPS
    ys = jnp.arange(tiles_y, dtype=jnp.int32)[:, None, None]
    xs = jnp.arange(tiles_x, dtype=jnp.int32)[None, :, None]
    places = (ys + tile_columns // 3) * (tiles_x + 2) + xs + tile_columns % 3
    present, field = pl.pallas_call(
        functools.partial(body, n_row, n_col, total, tiles_y, tiles_x, tile_count),
        out_shape=(
            jax.ShapeDtypeStruct((excite, shard), bf16),
            jax.ShapeDtypeStruct((count, excite, side), f32),
        ),
        in_specs=[pl.BlockSpec(memory_space=pltpu.SMEM)] + [pl.BlockSpec(memory_space=pltpu.HBM)] * 5,
        out_specs=(vmem, vmem),
        scratch_shapes=[
            pltpu.VMEM((excite, shard), bf16),
            pltpu.VMEM((3, shard), f32),
            pltpu.VMEM((1, shard), jnp.int32),
            pltpu.VMEM((count * side, shard), bf16),
            pltpu.VMEM((8, shard), f32),
            pltpu.VMEM((group, 8, shard), f32),
            pltpu.VMEM((depth, 8, shard), f32),
            pltpu.VMEM((9, 8, shard), f32),
            pltpu.VMEM((group * shard, 8), f32),
            pltpu.VMEM((group * shard, depth * shard), bf16),
            pltpu.VMEM((shard, count * side), bf16),
            pltpu.VMEM((shard, halo * side), bf16),
            pltpu.VMEM(volume_tiles.shape, bf16),
            pltpu.VMEM((steps, excite, shard), bf16),
            pltpu.VMEM((steps, group, excite, shard), bf16),
            pltpu.VMEM((steps, depth, excite, shard), bf16),
            pltpu.VMEM((steps, depth, excite, shard), bf16),
            pltpu.VMEM((steps, excite, shard), bf16),
            pltpu.VMEM((steps, 9, excite, shard), bf16),
            pltpu.VMEM((count, excite, side), f32),
            pltpu.VMEM(((tiles_y + 2) * (tiles_x + 2), excite, side), bf16),
            pltpu.VMEM(((tiles_y + 2) * (tiles_x + 2), excite, side), bf16),
            pltpu.VMEM((steps, tiles_y + 2, tiles_x + 2, excite, side), bf16),
            pltpu.VMEM((steps, tiles_y, tiles_x, excite, side), bf16),
            pltpu.VMEM((excite, count * side), bf16),
            dma, dma((4,)), dma((group,)), dma((group,)), dma((depth,)), dma((depth,)), dma((9,)), dma((9,)),
            dma((steps, group)), dma((steps, group)), dma((steps, depth)), dma((steps, depth)),
            dma((steps, 9)), dma((steps, 9)), dma((steps, 9)), dma((steps, 9)),
        ],
        compiler_params=pltpu.CompilerParams(
            collective_id=0, has_side_effects=True, vmem_limit_bytes=60 * 2**20
        ),
        cost_estimate=pl.CostEstimate(flops=10**9, bytes_accessed=4 * 2**20, transcendentals=0),
    )(places.reshape(-1), traces, incident, points, coupling.reshape(1, shard), volume_tiles)
    field = field.reshape(tiles_y, tiles_x, excite, side).transpose(2, 0, 1, 3)
    return (present, field)


def solution(mesh):
    in_specs = (
        P(None, ("row", "col")),
        P(None, ("row", "col")),
        P(None, ("row", "col")),
        P(("row", "col")),
        P("row", "col", None, None, None),
        P("row", "col", None),
    )
    out_specs = (P(None, ("row", "col")), P(None, "row", "col", None))
    return jax.shard_map(
        functools.partial(per_device, mesh.shape["row"], mesh.shape["col"]),
        mesh=mesh, in_specs=in_specs, out_specs=out_specs, check_vma=False,
    )
```
